32 devices in a mesh: rows: 4 (over z), seq: 8 (over y, x, core).
Axes of the slice: x: 2, y: 2, z: 4, core: 2. Of those that a mesh axis runs over, the one named last changes fastest.
Arguments:
- queries: bfloat16 [2048, 4096], P('seq'), may hold values from -50 to 50
- keys: bfloat16 [2048, 4096], P('seq'), may hold values from -6 to 6
- values: bfloat16 [2048, 4096], P('seq'), may hold values from -6 to 6
- grad_out: bfloat16 [4, 2048, 4096], P('rows', 'seq'), may hold values from -6 to 6
- table: bfloat16 [33, 4096], replicated, may hold values from -6 to 6
- positions: int32 [4], P('rows'), may hold values from 0 to 2047
- residues: int32 [4], P('rows'), may hold values from 4 to 23
- tiles: int32 [16, 8], replicated, may hold values from 0 to 15, as said below
- counts: int32 [16], replicated, may hold values from 1 to 8, as said below
Outputs:
- grad_queries: bfloat16 [4, 2048, 4096], P('rows', 'seq')
- grad_keys: bfloat16 [4, 2048, 4096], P('rows', 'seq')
- grad_values: bfloat16 [4, 2048, 4096], P('rows', 'seq')
The draws below stay inside these ranges and needn't reach their ends.
Inputs may be any that keep to these rules, and one draw needn't show every extreme that they name: `tiles`: row i lists key blocks: entry 0 is i itself, the others differ from i and from each other. Only the first counts[i] entries of row i of tiles are used; some query block uses all 8.
All inputs are finite; a program needn't handle non-finite values.
Results may differ from the reference program's by a relative error of at most 0.0085.
Values may be sent and summed in bfloat16 or wider, within the bound.
A program may use at most 128 MiB of HBM per device.

```python
import jax
import jax.numpy as jnp
from jax import lax

HEADS = 32
D_HEAD = 128
VOCAB = 33
BLOCK = 128
TILES = 8
SEQ = 2048
ROWS = 4
D = 4096


def query_key_pair(key):
    base = jax.random.fold_in(key, 11)
    first_key, second_key = jax.random.split(base, 2)
    keys = jnp.clip(jax.random.normal(second_key, (SEQ, D)), -6.0, 6.0)
    queries = jnp.clip(jax.random.normal(first_key, (SEQ, D)), -6.0, 6.0)
    return (queries, keys)


def draw_queries(key, part):
    return query_key_pair(key)[0].astype(jnp.bfloat16)


def draw_keys(key, part):
    return query_key_pair(key)[1].astype(jnp.bfloat16)


def draw_tiles(key, part):
    block_count = SEQ // BLOCK
    scores = jax.random.randint(jax.random.fold_in(key, 3), (block_count, block_count - 1), 0, 1 << 20) * block_count
    scores = scores + jnp.arange(block_count - 1, dtype=jnp.int32)[None, :]
    order = jnp.argsort(scores, axis=1)
    offsets = order[:, :TILES - 1] + 1
    own = jnp.arange(block_count, dtype=jnp.int32)[:, None]
    others = (own + offsets) % block_count
    return jnp.concatenate([own, others], axis=1).astype(jnp.int32)


def draw_counts(key, part):
    block_count = SEQ // BLOCK
    first_key, second_key = jax.random.split(jax.random.fold_in(key, 5), 2)
    raw = jax.random.randint(first_key, (block_count,), 1, TILES + 1)
    fullest = jax.random.randint(second_key, (), 0, block_count)
    return jnp.where(jnp.arange(block_count) == fullest, TILES, raw).astype(jnp.int32)


def touch_ends(drawn, rng, low, largest):
    shape = drawn.shape
    spot = [jax.random.randint(jax.random.fold_in(rng, axis), (), 0, shape[axis]) for axis in range(len(shape))]
    drawn = drawn.at[tuple(spot)].set(low)
    longest = shape.index(max(shape))
    spot[longest] = (spot[longest] + 1) % shape[longest]
    return drawn.at[tuple(spot)].set(largest)


def block_scale(own_key, extent, shards, low, largest):
    gain, own = 1.0, jax.random.fold_in(own_key, 6)
    for position, blocks in shards:
        steps = jnp.exp(jax.random.uniform(jax.random.fold_in(own, position), (blocks,), jnp.float32, low / len(shards), largest / len(shards)))
        gain = gain * jnp.repeat(steps, extent[position] // blocks).reshape([-1 if axis == position else 1 for axis in range(len(extent))])
    return gain


def bell_draw(rng, dims, scale, reach, cuts=(), held_as=jnp.bfloat16):
    array = jax.random.normal(rng, dims, jnp.float32) * scale
    if len(cuts) > 0:
        array = block_scale(rng, dims, cuts, -0.22, 0.18) * array
    return jnp.clip(array, min=-reach, max=reach).astype(held_as)


def setup_inputs(seed: int = 0) -> dict:
    arg_keys = jax.random.split(jax.random.key(seed), 10)
    return {
        "queries": draw_queries(jax.random.fold_in(arg_keys[9], 71), 0),
        "keys": draw_keys(jax.random.fold_in(arg_keys[9], 71), 0),
        "values": bell_draw(arg_keys[2], (SEQ, D), 1.0, 6.0, ((0, 8),)),
        "grad_out": bell_draw(arg_keys[3], (ROWS, SEQ, D), 1.0, 6.0, ((0, 4), (1, 8))),
        "table": bell_draw(arg_keys[4], (VOCAB, D), 1.0, 6.0),
        "positions": touch_ends(jax.random.randint(arg_keys[5], (ROWS,), 0, SEQ), jax.random.fold_in(arg_keys[5], 1), 0, SEQ - 1).astype(jnp.int32),
        "residues": touch_ends(jax.random.randint(arg_keys[6], (ROWS,), 4, 24), jax.random.fold_in(arg_keys[6], 1), 4, 23).astype(jnp.int32),
        "tiles": draw_tiles(jax.random.fold_in(arg_keys[9], 71), 0),
        "counts": draw_counts(jax.random.fold_in(arg_keys[9], 71), 0),
    }


def substitute(grad_out, table, positions, residues, first_token):
    tok_count = grad_out.shape[1]
    spots = ((jnp.arange(tok_count, dtype=jnp.int32)[None, :] + first_token) == positions[:, None]).astype(jnp.float32)
    picks = (jnp.arange(table.shape[0], dtype=jnp.int32)[None, :] == residues[:, None]).astype(jnp.bfloat16)
    added = jnp.dot(picks, table, preferred_element_type=jnp.float32)
    summed = grad_out.astype(jnp.float32) + spots[:, :, None] * added[:, None, :]
    return summed.astype(jnp.bfloat16)


def log_total(scores):
    row_max = jnp.max(scores, axis=(-2, -1), keepdims=True)
    return row_max + jnp.log(jnp.sum(jnp.exp(scores - row_max), axis=(-2, -1), keepdims=True))


def reference(queries, keys, values, grad_out, table, positions, residues, tiles, counts):
    softmax_scale = D_HEAD ** -0.5
    block_count = SEQ // BLOCK
    cotangent = substitute(grad_out, table, positions, residues, 0)
    query_blocks = queries.reshape(block_count, BLOCK, HEADS, D_HEAD).astype(jnp.float32)
    key_blocks = keys.reshape(block_count, BLOCK, HEADS, D_HEAD).astype(jnp.float32)
    value_blocks = values.reshape(block_count, BLOCK, HEADS, D_HEAD).astype(jnp.float32)
    cot_blocks = cotangent.reshape(ROWS, block_count, BLOCK, HEADS, D_HEAD)
    slot_ids = jnp.arange(TILES, dtype=jnp.int32)

    def step(totals, block_index):
        grad_keys, grad_values = totals
        key_ids = tiles[block_index]
        live_slots = (slot_ids < counts[block_index])[None, None, :, None]
        query_now = query_blocks[block_index]
        key_tiles = key_blocks[key_ids]
        value_tiles = value_blocks[key_ids]
        cot_now = lax.dynamic_index_in_dim(cot_blocks, block_index, 1, keepdims=False).astype(jnp.float32)
        scores = jnp.einsum("qhd,tkhd->hqtk", query_now, key_tiles) * softmax_scale
        scores = jnp.where(live_slots, scores, -1e30)
        probs = jnp.where(live_slots, jnp.exp(scores - log_total(scores)), 0.0)
        probs_bf = lax.optimization_barrier(probs.astype(jnp.bfloat16)).astype(jnp.float32)
        grad_probs = jnp.einsum("rqhd,tkhd->rhqtk", cot_now, value_tiles)
        delta = jnp.sum(probs[None] * grad_probs, axis=(3, 4), keepdims=True)
        grad_scores = lax.optimization_barrier((probs[None] * (grad_probs - delta)).astype(jnp.bfloat16)).astype(jnp.float32)
        grad_query = (softmax_scale * jnp.einsum("rhqtk,tkhd->rqhd", grad_scores, key_tiles)).astype(jnp.bfloat16)
        key_terms = softmax_scale * jnp.einsum("rhqtk,qhd->rtkhd", grad_scores, query_now)
        value_terms = jnp.einsum("hqtk,rqhd->rtkhd", probs_bf, cot_now)
        grad_keys = grad_keys.at[:, key_ids].add(key_terms)
        grad_values = grad_values.at[:, key_ids].add(value_terms)
        return (grad_keys, grad_values), grad_query

    zeros_full = jnp.zeros((ROWS, block_count, BLOCK, HEADS, D_HEAD), jnp.float32)
    (grad_keys, grad_values), grad_query = lax.scan(step, (zeros_full, zeros_full), jnp.arange(block_count, dtype=jnp.int32))
    grad_queries = grad_query.transpose(1, 0, 2, 3, 4).reshape(ROWS, SEQ, D)
    grad_keys = grad_keys.reshape(ROWS, SEQ, D).astype(jnp.bfloat16)
    grad_values = grad_values.reshape(ROWS, SEQ, D).astype(jnp.bfloat16)
    return (grad_queries, grad_keys, grad_values)
```

```python
import functools

import jax
import jax.numpy as jnp
from jax import lax
from jax.experimental import pallas as pl
from jax.experimental.pallas import tpu as pltpu
from jax.sharding import PartitionSpec as P

D_HEAD = 128
BLOCK = 128
CHUNKS = 2
NEG = -1e30
VMEM_LIMIT = 56 * 1024 * 1024


def pack_kernel(heads, spot_ref, q_ref, k_ref, v_ref, g_ref, table_ref, out_ref):
    for a, ref in enumerate((q_ref, k_ref, v_ref)):
        for h in range(heads):
            out_ref[0, a, h] = ref[:, h * D_HEAD : (h + 1) * D_HEAD]
    tok_count = q_ref.shape[0]
    here = spot_ref[0]
    added = table_ref[pl.ds(spot_ref[1], 1), :]
    rows = lax.broadcasted_iota(jnp.int32, (tok_count, 1), 0)
    for h in range(heads):
        cols = slice(h * D_HEAD, (h + 1) * D_HEAD)
        out_ref[0, 3, h] = g_ref[0, :, cols]

    @pl.when((here >= 0) & (here < tok_count))
    def substitute():
        for h in range(heads):
            cols = slice(h * D_HEAD, (h + 1) * D_HEAD)
            term = jnp.where(rows == here, added[:, cols], 0.0)
            out_ref[0, 3, h] = (g_ref[0, :, cols].astype(jnp.float32) + term).astype(jnp.bfloat16)


def pack(chunk, devices, heads, spot, queries, keys, values, grad_out, table):
    tok_count = queries.shape[0]
    width = heads * D_HEAD
    wide = pl.BlockSpec((tok_count, width), lambda d, s: (0, d * CHUNKS + chunk))
    return pl.pallas_call(
        functools.partial(pack_kernel, heads),
        grid_spec=pltpu.PrefetchScalarGridSpec(
            num_scalar_prefetch=1,
            grid=(devices,),
            in_specs=[
                wide,
                wide,
                wide,
                pl.BlockSpec((1, tok_count, width), lambda d, s: (0, 0, d * CHUNKS + chunk)),
                pl.BlockSpec((table.shape[0], width), lambda d, s: (0, d * CHUNKS + chunk)),
            ],
            out_specs=pl.BlockSpec(
                (1, 4, heads, tok_count, D_HEAD), lambda d, s: (d, 0, 0, 0, 0)
            ),
        ),
        out_shape=jax.ShapeDtypeStruct((devices, 4, heads, tok_count, D_HEAD), jnp.bfloat16),
        compiler_params=pltpu.CompilerParams(vmem_limit_bytes=VMEM_LIMIT),
        cost_estimate=pl.CostEstimate(
            flops=0, bytes_accessed=16 * devices * heads * tok_count * D_HEAD, transcendentals=0
        ),
        name="pack",
    )(spot, queries, keys, values, grad_out, table)


def attend_kernel(heads, block_total, slots, per, tiles_ref, counts_ref, x_ref, out_ref, kt_ref, dk_ref, dv_ref):
    scale = D_HEAD ** (-0.5)
    nt = (((1,), (1,)), ((), ()))
    nn = (((1,), (0,)), ((), ()))
    dk_ref[...] = jnp.zeros_like(dk_ref)
    dv_ref[...] = jnp.zeros_like(dv_ref)

    def rows_of(block):
        return block // per, pl.ds(pl.multiple_of((block % per) * BLOCK, BLOCK), BLOCK)

    def turn(block, carry):
        dev, rows = rows_of(block)
        for h in range(heads):
            kt_ref[h, block] = x_ref[dev, 1, h, rows, :].astype(jnp.float32).T.astype(jnp.bfloat16)
        return carry

    lax.fori_loop(0, block_total, turn, 0)

    def attend(block, used):
        count = counts_ref[block]
        dev, rows = rows_of(block)
        listed = [tiles_ref[block, j] for j in range(used)]
        places = [rows_of(t) for t in listed]
        for h in range(heads):
            q = x_ref[dev, 0, h, rows, :]
            cot = x_ref[dev, 3, h, rows, :]
            ks = jnp.concatenate([x_ref[d, 1, h, r, :] for d, r in places], axis=0)
            vs = jnp.concatenate([x_ref[d, 2, h, r, :] for d, r in places], axis=0)
            kts = jnp.concatenate([kt_ref[h, t] for t in listed], axis=1)
            scores = lax.dot_general(ks, q, nt, preferred_element_type=jnp.float32)
            if used > 1:
                last = jnp.where(count >= used, scores[(used - 1) * BLOCK :], NEG)
                scores = jnp.concatenate([scores[: (used - 1) * BLOCK], last], axis=0)
            row_max = jnp.max(scores, axis=0, keepdims=True)
            weights = jnp.exp((scores - row_max) * scale)
            probs = weights * (1.0 / jnp.sum(weights, axis=0, keepdims=True))
            grad_probs = lax.dot_general(vs, cot, nt, preferred_element_type=jnp.float32)
            delta = jnp.sum(probs * grad_probs, axis=0, keepdims=True)
            grad_scores = (probs * (grad_probs - delta)).astype(jnp.bfloat16)
            value_terms = lax.dot_general(
                probs.astype(jnp.bfloat16), cot, nn, preferred_element_type=jnp.float32
            )
            key_terms = lax.dot_general(grad_scores, q, nn, preferred_element_type=jnp.float32)
            query_t = lax.dot_general(kts, grad_scores, nn, preferred_element_type=jnp.float32)
            out_ref[dev, 0, h, rows, :] = (scale * query_t.T).astype(jnp.bfloat16)
            for j, t in enumerate(listed):
                part = slice(j * BLOCK, (j + 1) * BLOCK)
                dv_ref[h, t] += value_terms[part]
                dk_ref[h, t] += key_terms[part]

    sizes = list(range(2, slots + 1, 2))

    def step(block, carry):
        count = counts_ref[block]
        for used in sizes:

            @pl.when((count <= used) & (count > used - 2))
            def run(used=used):
                attend(block, used)

        return carry

    lax.fori_loop(0, block_total, step, 0)

    def close(block, carry):
        dev, rows = rows_of(block)
        for h in range(heads):
            out_ref[dev, 1, h, rows, :] = (scale * dk_ref[h, block]).astype(jnp.bfloat16)
            out_ref[dev, 2, h, rows, :] = dv_ref[h, block].astype(jnp.bfloat16)
        return carry

    lax.fori_loop(0, block_total, close, 0)


def attend(tiles, counts, packed):
    devices, _, heads, tok_count, _ = packed.shape
    block_total, slots = tiles.shape
    per = tok_count // BLOCK
    vmem = pl.BlockSpec(memory_space=pltpu.VMEM)
    smem = pl.BlockSpec(memory_space=pltpu.SMEM)
    return pl.pallas_call(
        functools.partial(attend_kernel, heads, block_total, slots, per),
        in_specs=[smem, smem, vmem],
        out_specs=vmem,
        out_shape=jax.ShapeDtypeStruct((devices, 3, heads, tok_count, D_HEAD), jnp.bfloat16),
        scratch_shapes=[
            pltpu.VMEM((heads, block_total, D_HEAD, BLOCK), jnp.bfloat16),
            pltpu.VMEM((heads, block_total, BLOCK, D_HEAD), jnp.float32),
            pltpu.VMEM((heads, block_total, BLOCK, D_HEAD), jnp.float32),
        ],
        compiler_params=pltpu.CompilerParams(vmem_limit_bytes=VMEM_LIMIT),
        cost_estimate=pl.CostEstimate(
            flops=40 * heads * block_total * slots * BLOCK * BLOCK * D_HEAD,
            bytes_accessed=2 * 7 * heads * devices * tok_count * D_HEAD,
            transcendentals=heads * block_total * slots * BLOCK * BLOCK,
        ),
        name="attend",
    )(tiles, counts, packed)


def unpack_kernel(heads, *refs):
    ins, outs = refs[:CHUNKS], refs[CHUNKS:]
    for a, out in enumerate(outs):
        for c, ref in enumerate(ins):
            for h in range(heads):
                at = (c * heads + h) * D_HEAD
                out[0, :, at : at + D_HEAD] = ref[0, a, h]


def unpack(parts):
    devices, _, heads, tok_count, _ = parts[0].shape
    width = CHUNKS * heads * D_HEAD
    shape = jax.ShapeDtypeStruct((1, tok_count, devices * width), jnp.bfloat16)
    return pl.pallas_call(
        functools.partial(unpack_kernel, heads),
        grid=(devices,),
        in_specs=[pl.BlockSpec((1, 3, heads, tok_count, D_HEAD), lambda d: (d, 0, 0, 0, 0))] * CHUNKS,
        out_specs=[pl.BlockSpec((1, tok_count, width), lambda d: (0, 0, d))] * 3,
        out_shape=[shape] * 3,
        compiler_params=pltpu.CompilerParams(vmem_limit_bytes=VMEM_LIMIT),
        name="unpack",
    )(*parts)


def per_device(queries, keys, values, grad_out, table, positions, residues, tiles, counts):
    devices = lax.axis_size("seq")
    tok_count, width = queries.shape
    heads = width // D_HEAD // devices // CHUNKS
    spot = jnp.concatenate([positions - lax.axis_index("seq") * tok_count, residues])
    table32 = table.astype(jnp.float32)
    received = []
    for chunk in range(CHUNKS):
        packed = pack(chunk, devices, heads, spot, queries, keys, values, grad_out, table32)
        received.append(lax.all_to_all(packed, "seq", split_axis=0, concat_axis=0, tiled=True))
    parts = []
    for chunk in range(CHUNKS):
        grads = attend(tiles, counts, received[chunk])
        parts.append(lax.all_to_all(grads, "seq", split_axis=0, concat_axis=0, tiled=True))
    return tuple(unpack(parts))


def solution(mesh):
    placed = (
        P("seq", None),
        P("seq", None),
        P("seq", None),
        P("rows", "seq", None),
        P(),
        P("rows"),
        P("rows"),
        P(),
        P(),
    )
    return jax.shard_map(
        per_device,
        mesh=mesh,
        in_specs=placed,
        out_specs=(P("rows", "seq", None), P("rows", "seq", None), P("rows", "seq", None)),
        check_vma=False,
    )
```

```python
import functools

import jax
import jax.numpy as jnp
from jax import lax
from jax.experimental import pallas as pl
from jax.experimental.pallas import tpu as pltpu
from jax.sharding import PartitionSpec as P

D_HEAD = 128
BLOCK = 128
NEG = -1e30
LOG2E = 1.4426950408889634
VMEM_LIMIT = 60 * 1024 * 1024
MESH = pl.DeviceIdType.MESH


def fused_kernel(
    n,
    heads,
    pos_ref,
    bias_ref,
    added_ref,
    q_hbm,
    k_hbm,
    v_hbm,
    g_hbm,
    gq_hbm,
    gk_hbm,
    gv_hbm,
    recv,
    outs,
    kt_ref,
    s_ref,
    w_ref,
    dp_ref,
    dk_ref,
    dv_ref,
    in_send,
    in_recv,
    in_local,
    out_send,
    out_recv,
    out_local,
):
    me = lax.axis_index("seq")
    tok = q_hbm.shape[0]
    per = tok // BLOCK
    scale = D_HEAD ** (-0.5)
    nt = (((1,), (1,)), ((), ()))
    nn = (((1,), (0,)), ((), ()))
    results = (gq_hbm, gk_hbm, gv_hbm)

    def peer(step):
        return lax.rem(me + step, n)

    barrier = pltpu.get_barrier_semaphore()

    def greet(step, carry):
        pl.semaphore_signal(barrier, inc=1, device_id={"seq": peer(step)}, device_id_type=MESH)
        return carry

    lax.fori_loop(1, n, greet, 0)
    pl.semaphore_wait(barrier, n - 1)

    def columns(owner, h):
        return pl.ds(pl.multiple_of((owner * heads + h) * D_HEAD, D_HEAD), D_HEAD)

    def sources(cols):
        return (q_hbm.at[:, cols], k_hbm.at[:, cols], v_hbm.at[:, cols], g_hbm.at[0, :, cols])

    def send_in(h):
        def one(step, carry):
            to = peer(step)
            for a, src in enumerate(sources(columns(to, h))):
                pltpu.make_async_remote_copy(
                    src_ref=src,
                    dst_ref=recv.at[h, me, a],
                    send_sem=in_send.at[h],
                    recv_sem=in_recv.at[h],
                    device_id={"seq": to},
                    device_id_type=MESH,
                ).start()
            return carry

        lax.fori_loop(1, n, one, 0)
        for a, src in enumerate(sources(columns(me, h))):
            pltpu.make_async_copy(src, recv.at[h, me, a], in_local.at[h]).start()

    def wait_bytes(ref, sem):
        pltpu.make_async_copy(ref, ref, sem).wait()

    def wait_sent(h):
        wait_bytes(recv.at[h, pl.ds(0, n - 1)], in_send.at[h])

    def wait_in(h):
        wait_bytes(recv.at[h, pl.ds(0, n - 1)], in_recv.at[h])
        wait_bytes(recv.at[h, 0], in_local.at[h])

    def send_out(h):
        cols = columns(me, h)

        def one(step, carry):
            to = peer(step)
            for a, dst in enumerate(results):
                pltpu.make_async_remote_copy(
                    src_ref=outs.at[h, to, a],
                    dst_ref=dst.at[0, :, cols],
                    send_sem=out_send,
                    recv_sem=out_recv,
                    device_id={"seq": to},
                    device_id_type=MESH,
                ).start()
            return carry

        lax.fori_loop(1, n, one, 0)
        for a, dst in enumerate(results):
            pltpu.make_async_copy(outs.at[h, me, a], dst.at[0, :, cols], out_local).start()

    def attend(h):
        def turn(src, carry):
            kt_ref[src] = recv[h, src, 1].astype(jnp.float32).T.astype(jnp.bfloat16)
            return carry

        lax.fori_loop(0, n, turn, 0)
        dk_ref[...] = jnp.zeros_like(dk_ref)
        dv_ref[...] = jnp.zeros_like(dv_ref)
        added = added_ref[pl.ds(h, 1), :]

        def queries_of(src, carry):
            q = recv[h, src, 0]
            at = lax.broadcasted_iota(jnp.int32, (tok, D_HEAD), 0) + src * tok
            term = jnp.where(at == pos_ref[0], added, 0.0)
            cot = (recv[h, src, 3].astype(jnp.float32) + term).astype(jnp.bfloat16)
            top = jnp.full((1, tok), NEG, jnp.float32)
            for c in range(n):
                scores = lax.dot_general(recv[h, c, 1], q, nt, preferred_element_type=jnp.float32)
                for b in range(per):
                    part = scores[b * BLOCK : (b + 1) * BLOCK] + bias_ref[src, pl.ds(c * per + b, 1), :]
                    s_ref[c, b * BLOCK : (b + 1) * BLOCK, :] = part
                    top = jnp.maximum(top, jnp.max(part, axis=0, keepdims=True))
            total = jnp.zeros((1, tok), jnp.float32)
            delta = jnp.zeros((1, tok), jnp.float32)
            for c in range(n):
                weights = jnp.exp2((s_ref[c] - top) * (scale * LOG2E))
                grad_probs = lax.dot_general(
                    recv[h, c, 2], cot, nt, preferred_element_type=jnp.float32
                )
                w_ref[c] = weights
                dp_ref[c] = grad_probs
                total += jnp.sum(weights, axis=0, keepdims=True)
                delta += jnp.sum(weights * grad_probs, axis=0, keepdims=True)
            inverse = 1.0 / total
            delta = delta * inverse
            query_t = jnp.zeros((D_HEAD, tok), jnp.float32)
            for c in range(n):
                probs = w_ref[c] * inverse
                grad_scores = (probs * (dp_ref[c] - delta)).astype(jnp.bfloat16)
                dv_ref[c] += lax.dot_general(
                    probs.astype(jnp.bfloat16), cot, nn, preferred_element_type=jnp.float32
                )
                dk_ref[c] += lax.dot_general(grad_scores, q, nn, preferred_element_type=jnp.float32)
                query_t += lax.dot_general(
                    kt_ref[c], grad_scores, nn, preferred_element_type=jnp.float32
                )
            outs[h, src, 0] = (scale * query_t.T).astype(jnp.bfloat16)
            return carry

        lax.fori_loop(0, n, queries_of, 0)

        def close(src, carry):
            outs[h, src, 1] = (scale * dk_ref[src]).astype(jnp.bfloat16)
            outs[h, src, 2] = dv_ref[src].astype(jnp.bfloat16)
            return carry

        lax.fori_loop(0, n, close, 0)

    send_in(0)
    wait_sent(0)
    if heads > 1:
        send_in(1)

    def turn_of(h, carry):
        wait_in(h)

        @pl.when(h + 2 < heads)
        def ahead():
            send_in(h + 2)

        attend(h)
        send_out(h)
        return carry

    lax.fori_loop(0, heads, turn_of, 0)
    for h in range(1, heads):
        wait_sent(h)
    wait_bytes(outs.at[:, pl.ds(0, n - 1)], out_send)
    wait_bytes(outs.at[:, pl.ds(0, n - 1)], out_recv)
    wait_bytes(outs.at[:, 0], out_local)


def per_device(queries, keys, values, grad_out, table, positions, residues, tiles, counts):
    n = lax.axis_size("seq")
    tok, width = queries.shape
    heads = width // D_HEAD // n
    block_total, slots = tiles.shape
    used = jnp.arange(slots, dtype=jnp.int32)[None, :] < counts[:, None]
    blocks = jnp.arange(block_total, dtype=jnp.int32)
    listed = jnp.any((tiles[:, :, None] == blocks) & used[:, :, None], axis=1)
    bias = jnp.where(listed, 0.0, NEG).astype(jnp.float32)
    bias = bias.reshape(n, tok // BLOCK, block_total).transpose(0, 2, 1)
    bias = jnp.repeat(bias, BLOCK, axis=2)
    own = lax.dynamic_slice(
        table, (residues[0], lax.axis_index("seq") * heads * D_HEAD), (1, heads * D_HEAD)
    )
    added = own.astype(jnp.float32).reshape(heads, D_HEAD)
    hbm = pl.BlockSpec(memory_space=pl.ANY)
    vmem = pl.BlockSpec(memory_space=pltpu.VMEM)
    shape = jax.ShapeDtypeStruct((1, tok, width), jnp.bfloat16)
    return pl.pallas_call(
        functools.partial(fused_kernel, n, heads),
        in_specs=[pl.BlockSpec(memory_space=pltpu.SMEM), vmem, vmem, hbm, hbm, hbm, hbm],
        out_specs=[hbm] * 3,
        out_shape=[shape] * 3,
        scratch_shapes=[
            pltpu.VMEM((heads, n, 4, tok, D_HEAD), jnp.bfloat16),
            pltpu.VMEM((heads, n, 3, tok, D_HEAD), jnp.bfloat16),
            pltpu.VMEM((n, D_HEAD, tok), jnp.bfloat16),
            pltpu.VMEM((n, tok, tok), jnp.float32),
            pltpu.VMEM((n, tok, tok), jnp.float32),
            pltpu.VMEM((n, tok, tok), jnp.float32),
            pltpu.VMEM((n, tok, D_HEAD), jnp.float32),
            pltpu.VMEM((n, tok, D_HEAD), jnp.float32),
            pltpu.SemaphoreType.DMA((heads,)),
            pltpu.SemaphoreType.DMA((heads,)),
            pltpu.SemaphoreType.DMA((heads,)),
            pltpu.SemaphoreType.DMA,
            pltpu.SemaphoreType.DMA,
            pltpu.SemaphoreType.DMA,
        ],
        compiler_params=pltpu.CompilerParams(
            vmem_limit_bytes=VMEM_LIMIT, collective_id=0, has_side_effects=True
        ),
        name="fused",
    )(positions, bias, added, queries, keys, values, grad_out)


def solution(mesh):
    placed = (
        P("seq", None),
        P("seq", None),
        P("seq", None),
        P("rows", "seq", None),
        P(),
        P("rows"),
        P("rows"),
        P(),
        P(),
    )
    return jax.shard_map(
        per_device,
        mesh=mesh,
        in_specs=placed,
        out_specs=(P("rows", "seq", None), P("rows", "seq", None), P("rows", "seq", None)),
        check_vma=False,
    )
```

```python
import functools

import jax
import jax.numpy as jnp
from jax import lax
from jax.experimental import pallas as pl
from jax.experimental.pallas import tpu as pltpu
from jax.sharding import PartitionSpec as P

D_HEAD = 128
BLOCK = 128
NEG = -1e30
LOG2E = 1.4426950408889634
VMEM_LIMIT = 60 * 1024 * 1024
MESH = pl.DeviceIdType.MESH


def fused_kernel(
    n,
    heads,
    pos_ref,
    residue_ref,
    tiles_ref,
    counts_ref,
    table_ref,
    q_hbm,
    k_hbm,
    v_hbm,
    g_hbm,
    gq_hbm,
    gk_hbm,
    gv_hbm,
    recv,
    outs,
    bias_ref,
    kt_ref,
    vt_ref,
    s_ref,
    w_ref,
    dk_ref,
    dv_ref,
    in_send,
    in_recv,
    in_local,
    out_send,
    out_recv,
    out_local,
):
    me = lax.axis_index("seq")
    tok = q_hbm.shape[0]
    per = tok // BLOCK
    scale = D_HEAD ** (-0.5)
    nt = (((1,), (1,)), ((), ()))
    nn = (((1,), (0,)), ((), ()))
    results = (gq_hbm, gk_hbm, gv_hbm)

    def peer(step):
        return lax.rem(me + step, n)

    barrier = pltpu.get_barrier_semaphore()

    def greet(step, carry):
        pl.semaphore_signal(barrier, inc=1, device_id={"seq": peer(step)}, device_id_type=MESH)
        return carry

    lax.fori_loop(1, n, greet, 0)
    pl.semaphore_wait(barrier, n - 1)

    def columns(owner, h):
        return pl.ds(pl.multiple_of((owner * heads + h) * D_HEAD, D_HEAD), D_HEAD)

    def sources(cols):
        return (q_hbm.at[:, cols], k_hbm.at[:, cols], v_hbm.at[:, cols], g_hbm.at[0, :, cols])

    def send_in(h):
        def one(step, carry):
            to = peer(step)
            for a, src in enumerate(sources(columns(to, h))):
                pltpu.make_async_remote_copy(
                    src_ref=src,
                    dst_ref=recv.at[h, me, a],
                    send_sem=in_send.at[h],
                    recv_sem=in_recv.at[h],
                    device_id={"seq": to},
                    device_id_type=MESH,
                ).start()
            return carry

        lax.fori_loop(1, n, one, 0)
        for a, src in enumerate(sources(columns(me, h))):
            pltpu.make_async_copy(src, recv.at[h, me, a], in_local.at[h]).start()

    def wait_bytes(ref, sem):
        pltpu.make_async_copy(ref, ref, sem).wait()

    def wait_sent(h):
        wait_bytes(recv.at[h, pl.ds(0, n - 1)], in_send.at[h])

    def wait_in(h):
        wait_bytes(recv.at[h, pl.ds(0, n - 1)], in_recv.at[h])
        wait_bytes(recv.at[h, 0], in_local.at[h])

    def send_out(h):
        cols = columns(me, h)

        def one(step, carry):
            to = peer(step)
            for a, dst in enumerate(results):
                pltpu.make_async_remote_copy(
                    src_ref=outs.at[h, to, a],
                    dst_ref=dst.at[0, :, cols],
                    send_sem=out_send,
                    recv_sem=out_recv,
                    device_id={"seq": to},
                    device_id_type=MESH,
                ).start()
            return carry

        lax.fori_loop(1, n, one, 0)
        for a, dst in enumerate(results):
            pltpu.make_async_copy(outs.at[h, me, a], dst.at[0, :, cols], out_local).start()

    def attend(h):
        def turn(src, carry):
            kt_ref[src] = recv[h, src, 1].T
            vt_ref[src] = recv[h, src, 2].T
            return carry

        lax.fori_loop(0, n, turn, 0)
        dk_ref[...] = jnp.zeros_like(dk_ref)
        dv_ref[...] = jnp.zeros_like(dv_ref)
        rows = table_ref[:, columns(me, h)].astype(jnp.float32)
        picked = lax.broadcasted_iota(jnp.int32, rows.shape, 0) == residue_ref[0]
        added = jnp.sum(jnp.where(picked, rows, 0.0), axis=0, keepdims=True)

        def queries_of(src, carry):
            q = recv[h, src, 0]
            at = lax.broadcasted_iota(jnp.int32, (tok, D_HEAD), 0) + src * tok
            term = jnp.where(at == pos_ref[0], added, 0.0)
            cot = (recv[h, src, 3].astype(jnp.float32) + term).astype(jnp.bfloat16)
            top = jnp.full((1, tok), NEG, jnp.float32)
            for c in range(n):
                scores = lax.dot_general(recv[h, c, 1], q, nt, preferred_element_type=jnp.float32)
                for b in range(per):
                    part = scores[b * BLOCK : (b + 1) * BLOCK] + bias_ref[src, pl.ds(c * per + b, 1), :]
                    s_ref[c, b * BLOCK : (b + 1) * BLOCK, :] = part
                    top = jnp.maximum(top, jnp.max(part, axis=0, keepdims=True))
            total = jnp.zeros((1, tok), jnp.float32)
            attended = jnp.zeros((D_HEAD, tok), jnp.float32)
            for c in range(n):
                weights = jnp.exp2((s_ref[c] - top) * (scale * LOG2E))
                total += jnp.sum(weights, axis=0, keepdims=True)
                weights_bf = weights.astype(jnp.bfloat16)
                w_ref[c] = weights_bf
                attended += lax.dot_general(
                    vt_ref[c], weights_bf, nn, preferred_element_type=jnp.float32
                )
            inverse = 1.0 / total
            cot_t = (cot.astype(jnp.float32).T * inverse).astype(jnp.bfloat16)
            cot_wide = cot_t.astype(jnp.float32)
            scaled = cot_wide.T.astype(jnp.bfloat16)
            delta = inverse * jnp.sum(cot_wide * attended, axis=0, keepdims=True)
            query_t = jnp.zeros((D_HEAD, tok), jnp.float32)
            for c in range(n):
                grad_probs = lax.dot_general(
                    recv[h, c, 2], cot_t, nn, preferred_element_type=jnp.float32
                )
                weights_bf = w_ref[c]
                grad_scores = weights_bf * (grad_probs - delta).astype(jnp.bfloat16)
                dv_ref[c] += lax.dot_general(
                    weights_bf, scaled, nn, preferred_element_type=jnp.float32
                )
                dk_ref[c] += lax.dot_general(grad_scores, q, nn, preferred_element_type=jnp.float32)
                query_t += lax.dot_general(
                    kt_ref[c], grad_scores, nn, preferred_element_type=jnp.float32
                )
            outs[h, src, 0] = (scale * query_t.T).astype(jnp.bfloat16)
            return carry

        lax.fori_loop(0, n, queries_of, 0)

        def close(src, carry):
            outs[h, src, 1] = (scale * dk_ref[src]).astype(jnp.bfloat16)
            outs[h, src, 2] = dv_ref[src].astype(jnp.bfloat16)
            return carry

        lax.fori_loop(0, n, close, 0)

    def mask_of(src, carry):
        for p in range(per):
            block = src * per + p
            ids = lax.broadcasted_iota(jnp.int32, (bias_ref.shape[1], BLOCK), 0)
            hit = ids == tiles_ref[block, 0]
            for j in range(1, tiles_ref.shape[1]):
                hit |= ids == jnp.where(j < counts_ref[block], tiles_ref[block, j], -1)
            bias_ref[src, :, p * BLOCK : (p + 1) * BLOCK] = jnp.where(hit, 0.0, NEG)
        return carry

    send_in(0)
    lax.fori_loop(0, n, mask_of, 0)
    wait_sent(0)
    if heads > 1:
        send_in(1)

    def turn_of(h, carry):
        wait_in(h)

        @pl.when(h + 2 < heads)
        def ahead():
            send_in(h + 2)

        attend(h)
        send_out(h)
        return carry

    lax.fori_loop(0, heads, turn_of, 0)
    for h in range(1, heads):
        wait_sent(h)
    wait_bytes(outs.at[:, pl.ds(0, n - 1)], out_send)
    wait_bytes(outs.at[:, pl.ds(0, n - 1)], out_recv)
    wait_bytes(outs.at[:, 0], out_local)


def per_device(queries, keys, values, grad_out, table, positions, residues, tiles, counts):
    n = lax.axis_size("seq")
    tok, width = queries.shape
    heads = width // D_HEAD // n
    block_total = tiles.shape[0]
    hbm = pl.BlockSpec(memory_space=pl.ANY)
    smem = pl.BlockSpec(memory_space=pltpu.SMEM)
    vmem = pl.BlockSpec(memory_space=pltpu.VMEM)
    shape = jax.ShapeDtypeStruct((1, tok, width), jnp.bfloat16)
    return pl.pallas_call(
        functools.partial(fused_kernel, n, heads),
        in_specs=[smem, smem, smem, smem, vmem, hbm, hbm, hbm, hbm],
        out_specs=[hbm] * 3,
        out_shape=[shape] * 3,
        scratch_shapes=[
            pltpu.VMEM((heads, n, 4, tok, D_HEAD), jnp.bfloat16),
            pltpu.VMEM((heads, n, 3, tok, D_HEAD), jnp.bfloat16),
            pltpu.VMEM((n, block_total, tok), jnp.float32),
            pltpu.VMEM((n, D_HEAD, tok), jnp.bfloat16),
            pltpu.VMEM((n, D_HEAD, tok), jnp.bfloat16),
            pltpu.VMEM((n, tok, tok), jnp.float32),
            pltpu.VMEM((n, tok, tok), jnp.bfloat16),
            pltpu.VMEM((n, tok, D_HEAD), jnp.float32),
            pltpu.VMEM((n, tok, D_HEAD), jnp.float32),
            pltpu.SemaphoreType.DMA((heads,)),
            pltpu.SemaphoreType.DMA((heads,)),
            pltpu.SemaphoreType.DMA((heads,)),
            pltpu.SemaphoreType.DMA,
            pltpu.SemaphoreType.DMA,
            pltpu.SemaphoreType.DMA,
        ],
        compiler_params=pltpu.CompilerParams(
            vmem_limit_bytes=VMEM_LIMIT, collective_id=0, has_side_effects=True
        ),
        name="fused",
    )(positions, residues, tiles, counts, table, queries, keys, values, grad_out)


def solution(mesh):
    placed = (
        P("seq", None),
        P("seq", None),
        P("seq", None),
        P("rows", "seq", None),
        P(),
        P("rows"),
        P("rows"),
        P(),
        P(),
    )
    return jax.shard_map(
        per_device,
        mesh=mesh,
        in_specs=placed,
        out_specs=(P("rows", "seq", None), P("rows", "seq", None), P("rows", "seq", None)),
        check_vma=False,
    )
```

```python
import functools

import jax
import jax.numpy as jnp
from jax import lax
from jax.experimental import pallas as pl
from jax.experimental.pallas import tpu as pltpu
from jax.sharding import PartitionSpec as P

D_HEAD = 128
BLOCK = 128
NEG = -1e30
LOG2E = 1.4426950408889634
VMEM_LIMIT = 60 * 1024 * 1024
MESH = pl.DeviceIdType.MESH


def fused_kernel(
    n,
    planes,
    heads,
    pos_ref,
    residue_ref,
    tiles_ref,
    counts_ref,
    table_ref,
    q_hbm,
    k_hbm,
    v_hbm,
    g_hbm,
    gq_hbm,
    gk_hbm,
    gv_hbm,
    recv,
    outs,
    bias_ref,
    kt_ref,
    vt_ref,
    s_ref,
    w_ref,
    dk_ref,
    dv_ref,
    in_send,
    in_recv,
    in_local,
    share_send,
    share_recv,
    plane_send,
    plane_recv,
    out_send,
    out_recv,
    out_local,
):
    me = lax.axis_index("seq")
    tok = q_hbm.shape[0]
    per = tok // BLOCK
    scale = D_HEAD ** (-0.5)
    nt = (((1,), (1,)), ((), ()))
    nn = (((1,), (0,)), ((), ()))
    results = (gq_hbm, gk_hbm, gv_hbm)

    plane = lax.axis_index("rows")
    share = tok // planes
    own_rows = pl.ds(pl.multiple_of(plane * share, share), share)
    core = lax.rem(me, 2)

    def peer(step):
        high, mid, low = step // 4, (step // 2) % 2, step % 2
        swapped = (high // 2) * 8 + mid * 4 + (high % 2) * 2 + low
        off = step + core * (swapped - step)
        return (
            ((me // 4 + off // 4) % (n // 4)) * 4
            + ((me // 2 + off // 2) % 2) * 2
            + (me + off) % 2
        )

    def other_plane(step):
        return lax.rem(plane + step, planes)

    barrier = pltpu.get_barrier_semaphore()

    def greet(step, carry):
        pl.semaphore_signal(barrier, inc=1, device_id={"seq": peer(step)}, device_id_type=MESH)
        return carry

    def greet_plane(step, carry):
        to = other_plane(step)
        pl.semaphore_signal(barrier, inc=1, device_id={"rows": to}, device_id_type=MESH)
        return carry

    lax.fori_loop(1, n, greet, 0)
    lax.fori_loop(1, planes, greet_plane, 0)
    pl.semaphore_wait(barrier, n - 1 + planes - 1)

    def columns(owner, h):
        return pl.ds(pl.multiple_of((owner * heads + h) * D_HEAD, D_HEAD), D_HEAD)

    def sources(cols):
        return (q_hbm.at[:, cols], k_hbm.at[:, cols], v_hbm.at[:, cols], g_hbm.at[0, :, cols])

    def send_in(h, first):
        def one(step, carry):
            to = peer(step)
            for a, src in enumerate(sources(columns(to, h))):
                if a >= first:
                    pltpu.make_async_remote_copy(
                        src_ref=src,
                        dst_ref=recv.at[h, me, a],
                        send_sem=in_send.at[h],
                        recv_sem=in_recv.at[h],
                        device_id={"seq": to},
                        device_id_type=MESH,
                    ).start()
            return carry

        lax.fori_loop(1, n, one, 0)
        for a, src in enumerate(sources(columns(me, h))):
            pltpu.make_async_copy(src, recv.at[h, me, a], in_local.at[h]).start()

    def send_share(h):
        def one(step, carry):
            to = peer(step)
            cols = columns(to, h)
            for a, src in enumerate((q_hbm, k_hbm, v_hbm)):
                pltpu.make_async_remote_copy(
                    src_ref=src.at[own_rows, cols],
                    dst_ref=recv.at[h, me, a, own_rows],
                    send_sem=share_send.at[h],
                    recv_sem=share_recv.at[h],
                    device_id={"seq": to},
                    device_id_type=MESH,
                ).start()
            return carry

        lax.fori_loop(1, n, one, 0)

    def share_bytes(h):
        return recv.at[h, pl.ds(0, n - 1), pl.ds(0, 3), pl.ds(0, share)]

    def plane_bytes(h):
        return recv.at[h, pl.ds(0, n - 1), pl.ds(0, 3), pl.ds(0, (planes - 1) * share)]

    def forward(h):
        wait_bytes(share_bytes(h), share_recv.at[h])

        def one(step, carry):
            block = recv.at[h, peer(step), pl.ds(0, 3), own_rows]

            def over(hop, inner):
                pltpu.make_async_remote_copy(
                    src_ref=block,
                    dst_ref=block,
                    send_sem=plane_send.at[h],
                    recv_sem=plane_recv.at[h],
                    device_id={"rows": other_plane(hop)},
                    device_id_type=MESH,
                ).start()
                return inner

            return lax.fori_loop(1, planes, over, carry)

        lax.fori_loop(1, n, one, 0)

    def wait_bytes(ref, sem):
        pltpu.make_async_copy(ref, ref, sem).wait()

    def wait_sent(h):
        first = 0 if h == 0 else 3
        wait_bytes(recv.at[h, pl.ds(0, n - 1), pl.ds(first, 4 - first)], in_send.at[h])

    def wait_in(h, first):
        wait_bytes(recv.at[h, 0], in_local.at[h])
        wait_bytes(recv.at[h, pl.ds(0, n - 1), pl.ds(first, 4 - first)], in_recv.at[h])

    def send_out(h):
        cols = columns(me, h)

        def one(step, carry):
            to = peer(step)
            for a, dst in enumerate(results):
                pltpu.make_async_remote_copy(
                    src_ref=outs.at[h, to, a],
                    dst_ref=dst.at[0, :, cols],
                    send_sem=out_send,
                    recv_sem=out_recv,
                    device_id={"seq": to},
                    device_id_type=MESH,
                ).start()
            return carry

        lax.fori_loop(1, n, one, 0)
        for a, dst in enumerate(results):
            pltpu.make_async_copy(outs.at[h, me, a], dst.at[0, :, cols], out_local).start()

    def attend(h):
        def turn(src, carry):
            kt_ref[src] = recv[h, src, 1].T
            vt_ref[src] = recv[h, src, 2].T
            return carry

        lax.fori_loop(0, n, turn, 0)
        dk_ref[...] = jnp.zeros_like(dk_ref)
        dv_ref[...] = jnp.zeros_like(dv_ref)
        rows = table_ref[:, columns(me, h)].astype(jnp.float32)
        picked = lax.broadcasted_iota(jnp.int32, rows.shape, 0) == residue_ref[0]
        added = jnp.sum(jnp.where(picked, rows, 0.0), axis=0, keepdims=True)

        def queries_of(src, carry):
            if heads > 2:

                @pl.when((h == 0) & (src == min(3, n - 1)))
                def onward():
                    for later in range(2, heads):
                        forward(later)

            q = recv[h, src, 0]
            at = lax.broadcasted_iota(jnp.int32, (tok, D_HEAD), 0) + src * tok
            term = jnp.where(at == pos_ref[0], added, 0.0)
            cot = (recv[h, src, 3].astype(jnp.float32) + term).astype(jnp.bfloat16)
            top = jnp.full((1, tok), NEG, jnp.float32)
            for c in range(n):
                scores = lax.dot_general(recv[h, c, 1], q, nt, preferred_element_type=jnp.float32)
                for b in range(per):
                    part = scores[b * BLOCK : (b + 1) * BLOCK] + bias_ref[src, pl.ds(c * per + b, 1), :]
                    s_ref[c, b * BLOCK : (b + 1) * BLOCK, :] = part
                    top = jnp.maximum(top, jnp.max(part, axis=0, keepdims=True))
            total = jnp.zeros((1, tok), jnp.float32)
            attended = jnp.zeros((D_HEAD, tok), jnp.float32)
            for c in range(n):
                weights = jnp.exp2((s_ref[c] - top) * (scale * LOG2E))
                total += jnp.sum(weights, axis=0, keepdims=True)
                weights_bf = weights.astype(jnp.bfloat16)
                w_ref[c] = weights_bf
                attended += lax.dot_general(
                    vt_ref[c], weights_bf, nn, preferred_element_type=jnp.float32
                )
            inverse = 1.0 / total
            cot_t = (cot.astype(jnp.float32).T * inverse).astype(jnp.bfloat16)
            cot_wide = cot_t.astype(jnp.float32)
            scaled = cot_wide.T.astype(jnp.bfloat16)
            delta = inverse * jnp.sum(cot_wide * attended, axis=0, keepdims=True)
            query_t = jnp.zeros((D_HEAD, tok), jnp.float32)
            for c in range(n):
                grad_probs = lax.dot_general(
                    recv[h, c, 2], cot_t, nn, preferred_element_type=jnp.float32
                )
                weights_bf = w_ref[c]
                grad_scores = weights_bf * (grad_probs - delta).astype(jnp.bfloat16)
                dv_ref[c] += lax.dot_general(
                    weights_bf, scaled, nn, preferred_element_type=jnp.float32
                )
                dk_ref[c] += lax.dot_general(grad_scores, q, nn, preferred_element_type=jnp.float32)
                query_t += lax.dot_general(
                    kt_ref[c], grad_scores, nn, preferred_element_type=jnp.float32
                )
            outs[h, src, 0] = (scale * query_t.T).astype(jnp.bfloat16)
            return carry

        lax.fori_loop(0, n, queries_of, 0)

        def close(src, carry):
            outs[h, src, 1] = (scale * dk_ref[src]).astype(jnp.bfloat16)
            outs[h, src, 2] = dv_ref[src].astype(jnp.bfloat16)
            return carry

        lax.fori_loop(0, n, close, 0)

    def mask_of(src, carry):
        for p in range(per):
            block = src * per + p
            ids = lax.broadcasted_iota(jnp.int32, (bias_ref.shape[1], BLOCK), 0)
            hit = ids == tiles_ref[block, 0]
            for j in range(1, tiles_ref.shape[1]):
                hit |= ids == jnp.where(j < counts_ref[block], tiles_ref[block, j], -1)
            bias_ref[src, :, p * BLOCK : (p + 1) * BLOCK] = jnp.where(hit, 0.0, NEG)
        return carry

    if heads > 1:
        send_share(1)
    send_in(0, 0)
    lax.fori_loop(0, n, mask_of, 0)
    if heads > 1:
        forward(1)
    wait_sent(0)
    for h in range(2, heads):
        send_share(h)
    for h in range(1, heads):
        send_in(h, 3)
    wait_in(0, 0)

    def turn_of(h, carry):
        @pl.when(h > 0)
        def arrived():
            wait_in(h, 3)
            wait_bytes(plane_bytes(h), plane_recv.at[h])

        attend(h)
        send_out(h)
        return carry

    lax.fori_loop(0, heads, turn_of, 0)
    for h in range(1, heads):
        wait_sent(h)
        wait_bytes(share_bytes(h), share_send.at[h])
        wait_bytes(plane_bytes(h), plane_send.at[h])
    wait_bytes(outs.at[:, pl.ds(0, n - 1)], out_send)
    wait_bytes(outs.at[:, pl.ds(0, n - 1)], out_recv)
    wait_bytes(outs.at[:, 0], out_local)


def per_device(queries, keys, values, grad_out, table, positions, residues, tiles, counts):
    n, planes = lax.axis_size("seq"), lax.axis_size("rows")
    tok, width = queries.shape
    heads = width // D_HEAD // n
    block_total = tiles.shape[0]
    hbm = pl.BlockSpec(memory_space=pl.ANY)
    smem = pl.BlockSpec(memory_space=pltpu.SMEM)
    vmem = pl.BlockSpec(memory_space=pltpu.VMEM)
    shape = jax.ShapeDtypeStruct((1, tok, width), jnp.bfloat16)
    return pl.pallas_call(
        functools.partial(fused_kernel, n, planes, heads),
        in_specs=[smem, smem, smem, smem, vmem, hbm, hbm, hbm, hbm],
        out_specs=[hbm] * 3,
        out_shape=[shape] * 3,
        scratch_shapes=[
            pltpu.VMEM((heads, n, 4, tok, D_HEAD), jnp.bfloat16),
            pltpu.VMEM((heads, n, 3, tok, D_HEAD), jnp.bfloat16),
            pltpu.VMEM((n, block_total, tok), jnp.float32),
            pltpu.VMEM((n, D_HEAD, tok), jnp.bfloat16),
            pltpu.VMEM((n, D_HEAD, tok), jnp.bfloat16),
            pltpu.VMEM((n, tok, tok), jnp.float32),
            pltpu.VMEM((n, tok, tok), jnp.bfloat16),
            pltpu.VMEM((n, tok, D_HEAD), jnp.float32),
            pltpu.VMEM((n, tok, D_HEAD), jnp.float32),
            pltpu.SemaphoreType.DMA((heads,)),
            pltpu.SemaphoreType.DMA((heads,)),
            pltpu.SemaphoreType.DMA((heads,)),
            pltpu.SemaphoreType.DMA((heads,)),
            pltpu.SemaphoreType.DMA((heads,)),
            pltpu.SemaphoreType.DMA((heads,)),
            pltpu.SemaphoreType.DMA((heads,)),
            pltpu.SemaphoreType.DMA,
            pltpu.SemaphoreType.DMA,
            pltpu.SemaphoreType.DMA,
        ],
        compiler_params=pltpu.CompilerParams(
            vmem_limit_bytes=VMEM_LIMIT, collective_id=0, has_side_effects=True
        ),
        name="fused",
    )(positions, residues, tiles, counts, table, queries, keys, values, grad_out)


def solution(mesh):
    placed = (
        P("seq", None),
        P("seq", None),
        P("seq", None),
        P("rows", "seq", None),
        P(),
        P("rows"),
        P("rows"),
        P(),
        P(),
    )
    return jax.shard_map(
        per_device,
        mesh=mesh,
        in_specs=placed,
        out_specs=(P("rows", "seq", None), P("rows", "seq", None), P("rows", "seq", None)),
        check_vma=False,
    )
```

```python
import functools
import math

import jax
import jax.numpy as jnp
from jax import lax
from jax.experimental import pallas as pl
from jax.experimental.pallas import tpu as pltpu
from jax.sharding import PartitionSpec as P

D_HEAD = 128
BLOCK = 128
NEG = -1e30
LOG2E = 1.4426950408889634
VMEM_LIMIT = 60 * 1024 * 1024
MESH = pl.DeviceIdType.MESH


def fused_kernel(
    n,
    planes,
    heads,
    pos_ref,
    residue_ref,
    tiles_ref,
    counts_ref,
    table_ref,
    q_hbm,
    k_hbm,
    v_hbm,
    g_hbm,
    gq_hbm,
    gk_hbm,
    gv_hbm,
    recv,
    outs,
    bias_ref,
    kt_ref,
    vt_ref,
    s_ref,
    w_ref,
    ds_ref,
    scaled_ref,
    dk_ref,
    dv_ref,
    in_send,
    in_recv,
    in_local,
    share_send,
    share_recv,
    plane_send,
    plane_recv,
    out_send,
    out_recv,
    out_local,
):
    me = lax.axis_index("seq")
    tok = q_hbm.shape[0]
    per = tok // BLOCK
    scale = D_HEAD ** (-0.5)
    nt = (((1,), (1,)), ((), ()))
    nn = (((1,), (0,)), ((), ()))
    batch = scaled_ref.shape[0] // tok

    plane = lax.axis_index("rows")
    share = tok // planes
    own_rows = pl.ds(pl.multiple_of(plane * share, share), share)
    core = lax.rem(me, 2)

    def peer(step):
        high, mid, low = step // 4, (step // 2) % 2, step % 2
        swapped = (high // 2) * 8 + mid * 4 + (high % 2) * 2 + low
        off = step + core * (swapped - step)
        return (
            ((me // 4 + off // 4) % (n // 4)) * 4
            + ((me // 2 + off // 2) % 2) * 2
            + (me + off) % 2
        )

    def other_plane(step):
        return lax.rem(plane + step, planes)

    barrier = pltpu.get_barrier_semaphore()

    def greet(step, carry):
        pl.semaphore_signal(barrier, inc=1, device_id={"seq": peer(step)}, device_id_type=MESH)
        return carry

    def greet_plane(step, carry):
        to = other_plane(step)
        pl.semaphore_signal(barrier, inc=1, device_id={"rows": to}, device_id_type=MESH)
        return carry

    lax.fori_loop(1, n, greet, 0)
    lax.fori_loop(1, planes, greet_plane, 0)
    pl.semaphore_wait(barrier, n - 1 + planes - 1)

    def columns(owner, h):
        return pl.ds(pl.multiple_of((owner * heads + h) * D_HEAD, D_HEAD), D_HEAD)

    def sources(cols):
        return (q_hbm.at[:, cols], k_hbm.at[:, cols], v_hbm.at[:, cols], g_hbm.at[0, :, cols])

    def send_in(h, first):
        def one(step, carry):
            to = peer(step)
            for a, src in enumerate(sources(columns(to, h))):
                if a >= first:
                    pltpu.make_async_remote_copy(
                        src_ref=src,
                        dst_ref=recv.at[h, me, a],
                        send_sem=in_send.at[h],
                        recv_sem=in_recv.at[h],
                        device_id={"seq": to},
                        device_id_type=MESH,
                    ).start()
            return carry

        lax.fori_loop(1, n, one, 0)
        for a, src in enumerate(sources(columns(me, h))):
            pltpu.make_async_copy(src, recv.at[h, me, a], in_local.at[h]).start()

    def send_share(h):
        def one(step, carry):
            to = peer(step)
            cols = columns(to, h)
            for a, src in enumerate((q_hbm, k_hbm, v_hbm)):
                pltpu.make_async_remote_copy(
                    src_ref=src.at[own_rows, cols],
                    dst_ref=recv.at[h, me, a, own_rows],
                    send_sem=share_send.at[h],
                    recv_sem=share_recv.at[h],
                    device_id={"seq": to},
                    device_id_type=MESH,
                ).start()
            return carry

        lax.fori_loop(1, n, one, 0)

    def share_bytes(h):
        return recv.at[h, pl.ds(0, n - 1), pl.ds(0, 3), pl.ds(0, share)]

    def plane_bytes(h):
        return recv.at[h, pl.ds(0, n - 1), pl.ds(0, 3), pl.ds(0, (planes - 1) * share)]

    def forward(h):
        wait_bytes(share_bytes(h), share_recv.at[h])

        def one(step, carry):
            block = recv.at[h, peer(step), pl.ds(0, 3), own_rows]

            def over(hop, inner):
                pltpu.make_async_remote_copy(
                    src_ref=block,
                    dst_ref=block,
                    send_sem=plane_send.at[h],
                    recv_sem=plane_recv.at[h],
                    device_id={"rows": other_plane(hop)},
                    device_id_type=MESH,
                ).start()
                return inner

            return lax.fori_loop(1, planes, over, carry)

        lax.fori_loop(1, n, one, 0)

    def wait_bytes(ref, sem):
        pltpu.make_async_copy(ref, ref, sem).wait()

    def wait_sent(h):
        first = 0 if h == 0 else 3
        wait_bytes(recv.at[h, pl.ds(0, n - 1), pl.ds(first, 4 - first)], in_send.at[h])

    def wait_in(h, first):
        wait_bytes(recv.at[h, 0], in_local.at[h])
        wait_bytes(recv.at[h, pl.ds(0, n - 1), pl.ds(first, 4 - first)], in_recv.at[h])

    def send_query(h, to):
        cols = columns(me, h)

        @pl.when(to != me)
        def away():
            pltpu.make_async_remote_copy(
                src_ref=outs.at[h, to, 0],
                dst_ref=gq_hbm.at[0, :, cols],
                send_sem=out_send,
                recv_sem=out_recv,
                device_id={"seq": to},
                device_id_type=MESH,
            ).start()

        @pl.when(to == me)
        def here():
            pltpu.make_async_copy(outs.at[h, to, 0], gq_hbm.at[0, :, cols], out_local).start()

    def send_out(h):
        cols = columns(me, h)

        def one(step, carry):
            to = peer(step)
            for a, dst in ((1, gk_hbm), (2, gv_hbm)):
                pltpu.make_async_remote_copy(
                    src_ref=outs.at[h, to, a],
                    dst_ref=dst.at[0, :, cols],
                    send_sem=out_send,
                    recv_sem=out_recv,
                    device_id={"seq": to},
                    device_id_type=MESH,
                ).start()
            return carry

        lax.fori_loop(1, n, one, 0)
        for a, dst in ((1, gk_hbm), (2, gv_hbm)):
            pltpu.make_async_copy(outs.at[h, me, a], dst.at[0, :, cols], out_local).start()

    def attend(h):
        def turn(src, carry):
            at = pl.ds(pl.multiple_of(src * tok, tok), tok)
            kt_ref[:, at] = recv[h, src, 1].T
            vt_ref[:, at] = recv[h, src, 2].T
            return carry

        lax.fori_loop(0, n, turn, 0)
        dk_ref[...] = jnp.zeros_like(dk_ref)
        dv_ref[...] = jnp.zeros_like(dv_ref)
        rows = table_ref[:, columns(me, h)].astype(jnp.float32)
        picked = lax.broadcasted_iota(jnp.int32, rows.shape, 0) == residue_ref[0]
        added = jnp.sum(jnp.where(picked, rows, 0.0), axis=0, keepdims=True)

        def queries_of(group, place):
            src = group * batch + place
            cols = pl.ds(pl.multiple_of(place * tok, tok), tok)
            if heads > 2:

                @pl.when((h == 0) & (src == min(3, n - 1)))
                def onward():
                    for later in range(2, heads):
                        forward(later)

            q = recv[h, src, 0]
            at = lax.broadcasted_iota(jnp.int32, (tok, D_HEAD), 0) + src * tok
            term = jnp.where(at == pos_ref[0], added, 0.0)
            cot = (recv[h, src, 3].astype(jnp.float32) + term).astype(jnp.bfloat16)
            top = jnp.full((8, tok), NEG, jnp.float32)
            for c in range(n):
                scores = lax.dot_general(recv[h, c, 1], q, nt, preferred_element_type=jnp.float32)
                for b in range(per):
                    part = scores[b * BLOCK : (b + 1) * BLOCK] + bias_ref[src, pl.ds(c * per + b, 1), :]
                    s_ref[c, b * BLOCK : (b + 1) * BLOCK, :] = part
                    top = jnp.maximum(top, jnp.max(part.reshape(BLOCK // 8, 8, tok), axis=0))
            top = jnp.max(top, axis=0, keepdims=True)
            total = jnp.zeros((8, tok), jnp.float32)
            for c in range(n):
                weights = jnp.exp2((s_ref[c] - top) * (scale * LOG2E))
                total += jnp.sum(weights.reshape(tok // 8, 8, tok), axis=0)
                w_ref[c, :, cols] = weights.astype(jnp.bfloat16)
            attended = lax.dot_general(
                vt_ref[...],
                w_ref[:, :, cols].reshape(n * tok, tok),
                nn,
                preferred_element_type=jnp.float32,
            )
            inverse = 1.0 / jnp.sum(total, axis=0, keepdims=True)
            cot_t = (cot.astype(jnp.float32).T * inverse).astype(jnp.bfloat16)
            cot_wide = cot_t.astype(jnp.float32)
            scaled_ref[cols, :] = cot_wide.T.astype(jnp.bfloat16)
            delta = inverse * jnp.sum(cot_wide * attended, axis=0, keepdims=True)
            for c in range(n):
                grad_probs = lax.dot_general(
                    recv[h, c, 2], cot_t, nn, preferred_element_type=jnp.float32
                )
                ds_ref[c, :, cols] = w_ref[c, :, cols] * (grad_probs - delta).astype(jnp.bfloat16)
            query_t = lax.dot_general(
                kt_ref[...],
                ds_ref[:, :, cols].reshape(n * tok, tok),
                nn,
                preferred_element_type=jnp.float32,
            )
            outs[h, src, 0] = (scale * query_t.T).astype(jnp.bfloat16)
            send_query(h, src)

        def batch_of(group, carry):
            def inner(place, unused):
                queries_of(group, place)
                return unused

            lax.fori_loop(0, batch, inner, 0)
            q_all = recv[h, pl.ds(group * batch, batch), 0].reshape(batch * tok, D_HEAD)
            cot_all = scaled_ref[...]

            def keys_of(c, unused):
                dv_ref[c] += lax.dot_general(
                    w_ref[c], cot_all, nn, preferred_element_type=jnp.float32
                )
                dk_ref[c] += lax.dot_general(ds_ref[c], q_all, nn, preferred_element_type=jnp.float32)
                return unused

            lax.fori_loop(0, n, keys_of, 0)
            return carry

        lax.fori_loop(0, n // batch, batch_of, 0)

        def close(src, carry):
            outs[h, src, 1] = (scale * dk_ref[src]).astype(jnp.bfloat16)
            outs[h, src, 2] = dv_ref[src].astype(jnp.bfloat16)
            return carry

        lax.fori_loop(0, n, close, 0)

    def mask_of(src, carry):
        for p in range(per):
            block = src * per + p
            ids = lax.broadcasted_iota(jnp.int32, (bias_ref.shape[1], BLOCK), 0)
            hit = ids == tiles_ref[block, 0]
            for j in range(1, tiles_ref.shape[1]):
                hit |= ids == jnp.where(j < counts_ref[block], tiles_ref[block, j], -1)
            bias_ref[src, :, p * BLOCK : (p + 1) * BLOCK] = jnp.where(hit, 0.0, NEG)
        return carry

    if heads > 1:
        send_share(1)
    send_in(0, 0)
    lax.fori_loop(0, n, mask_of, 0)
    if heads > 1:
        forward(1)
    wait_sent(0)
    for h in range(2, heads):
        send_share(h)
    for h in range(1, heads):
        send_in(h, 3)
    wait_in(0, 0)

    def turn_of(h, carry):
        @pl.when(h > 0)
        def arrived():
            wait_in(h, 3)
            wait_bytes(plane_bytes(h), plane_recv.at[h])

        attend(h)
        send_out(h)
        return carry

    lax.fori_loop(0, heads, turn_of, 0)
    for h in range(1, heads):
        wait_sent(h)
        wait_bytes(share_bytes(h), share_send.at[h])
        wait_bytes(plane_bytes(h), plane_send.at[h])
    wait_bytes(outs.at[:, pl.ds(0, n - 1)], out_send)
    wait_bytes(outs.at[:, pl.ds(0, n - 1)], out_recv)
    wait_bytes(outs.at[:, 0], out_local)


def per_device(queries, keys, values, grad_out, table, positions, residues, tiles, counts):
    n, planes = lax.axis_size("seq"), lax.axis_size("rows")
    tok, width = queries.shape
    heads = width // D_HEAD // n
    block_total = tiles.shape[0]
    batch = math.gcd(4, n)
    hbm = pl.BlockSpec(memory_space=pl.ANY)
    smem = pl.BlockSpec(memory_space=pltpu.SMEM)
    vmem = pl.BlockSpec(memory_space=pltpu.VMEM)
    shape = jax.ShapeDtypeStruct((1, tok, width), jnp.bfloat16)
    return pl.pallas_call(
        functools.partial(fused_kernel, n, planes, heads),
        in_specs=[smem, smem, smem, smem, vmem, hbm, hbm, hbm, hbm],
        out_specs=[hbm] * 3,
        out_shape=[shape] * 3,
        scratch_shapes=[
            pltpu.VMEM((heads, n, 4, tok, D_HEAD), jnp.bfloat16),
            pltpu.VMEM((heads, n, 3, tok, D_HEAD), jnp.bfloat16),
            pltpu.VMEM((n, block_total, tok), jnp.float32),
            pltpu.VMEM((D_HEAD, n * tok), jnp.bfloat16),
            pltpu.VMEM((D_HEAD, n * tok), jnp.bfloat16),
            pltpu.VMEM((n, tok, tok), jnp.float32),
            pltpu.VMEM((n, tok, batch * tok), jnp.bfloat16),
            pltpu.VMEM((n, tok, batch * tok), jnp.bfloat16),
            pltpu.VMEM((batch * tok, D_HEAD), jnp.bfloat16),
            pltpu.VMEM((n, tok, D_HEAD), jnp.float32),
            pltpu.VMEM((n, tok, D_HEAD), jnp.float32),
            pltpu.SemaphoreType.DMA((heads,)),
            pltpu.SemaphoreType.DMA((heads,)),
            pltpu.SemaphoreType.DMA((heads,)),
            pltpu.SemaphoreType.DMA((heads,)),
            pltpu.SemaphoreType.DMA((heads,)),
            pltpu.SemaphoreType.DMA((heads,)),
            pltpu.SemaphoreType.DMA((heads,)),
            pltpu.SemaphoreType.DMA,
            pltpu.SemaphoreType.DMA,
            pltpu.SemaphoreType.DMA,
        ],
        compiler_params=pltpu.CompilerParams(
            vmem_limit_bytes=VMEM_LIMIT, collective_id=0, has_side_effects=True
        ),
        name="fused",
    )(positions, residues, tiles, counts, table, queries, keys, values, grad_out)


def solution(mesh):
    placed = (
        P("seq", None),
        P("seq", None),
        P("seq", None),
        P("rows", "seq", None),
        P(),
        P("rows"),
        P("rows"),
        P(),
        P(),
    )
    return jax.shard_map(
        per_device,
        mesh=mesh,
        in_specs=placed,
        out_specs=(P("rows", "seq", None), P("rows", "seq", None), P("rows", "seq", None)),
        check_vma=False,
    )
```

```python
import functools
import math

import jax
import jax.numpy as jnp
from jax import lax
from jax.experimental import pallas as pl
from jax.experimental.pallas import tpu as pltpu
from jax.sharding import PartitionSpec as P

D_HEAD = 128
BLOCK = 128
NEG = -1e30
LOG2E = 1.4426950408889634
VMEM_LIMIT = 60 * 1024 * 1024
MESH = pl.DeviceIdType.MESH


def fused_kernel(
    n,
    planes,
    heads,
    pos_ref,
    residue_ref,
    tiles_ref,
    counts_ref,
    table_ref,
    q_hbm,
    k_hbm,
    v_hbm,
    g_hbm,
    gq_hbm,
    gk_hbm,
    gv_hbm,
    recv,
    outs,
    bias_ref,
    kt_ref,
    vt_ref,
    s_ref,
    w_ref,
    ds_ref,
    scaled_ref,
    q_ref,
    dk_ref,
    dv_ref,
    in_send,
    in_recv,
    in_local,
    share_send,
    share_recv,
    plane_send,
    plane_recv,
    out_send,
    out_recv,
    out_local,
):
    me = lax.axis_index("seq")
    tok = q_hbm.shape[0]
    per = tok // BLOCK
    scale = D_HEAD ** (-0.5)
    nt = (((1,), (1,)), ((), ()))
    nn = (((1,), (0,)), ((), ()))
    batch = scaled_ref.shape[0] // tok

    plane = lax.axis_index("rows")
    share = tok // planes
    own_rows = pl.ds(pl.multiple_of(plane * share, share), share)
    core = lax.rem(me, 2)

    def peer(step):
        high, mid, low = step // 4, (step // 2) % 2, step % 2
        swapped = (high // 2) * 8 + mid * 4 + (high % 2) * 2 + low
        off = step + core * (swapped - step)
        return (
            ((me // 4 + off // 4) % (n // 4)) * 4
            + ((me // 2 + off // 2) % 2) * 2
            + (me + off) % 2
        )

    def other_plane(step):
        return lax.rem(plane + step, planes)

    barrier = pltpu.get_barrier_semaphore()

    def greet(step, carry):
        pl.semaphore_signal(barrier, inc=1, device_id={"seq": peer(step)}, device_id_type=MESH)
        return carry

    def greet_plane(step, carry):
        to = other_plane(step)
        pl.semaphore_signal(barrier, inc=1, device_id={"rows": to}, device_id_type=MESH)
        return carry

    lax.fori_loop(1, n, greet, 0)
    lax.fori_loop(1, planes, greet_plane, 0)
    pl.semaphore_wait(barrier, n - 1 + planes - 1)

    def columns(owner, h):
        return pl.ds(pl.multiple_of((owner * heads + h) * D_HEAD, D_HEAD), D_HEAD)

    def sources(cols):
        return (q_hbm.at[:, cols], k_hbm.at[:, cols], v_hbm.at[:, cols], g_hbm.at[0, :, cols])

    def send_in(h, first):
        def one(step, carry):
            to = peer(step)
            for a, src in enumerate(sources(columns(to, h))):
                if a >= first:
                    pltpu.make_async_remote_copy(
                        src_ref=src,
                        dst_ref=recv.at[h, me, a],
                        send_sem=in_send.at[h],
                        recv_sem=in_recv.at[h],
                        device_id={"seq": to},
                        device_id_type=MESH,
                    ).start()
            return carry

        lax.fori_loop(1, n, one, 0)
        for a, src in enumerate(sources(columns(me, h))):
            pltpu.make_async_copy(src, recv.at[h, me, a], in_local.at[h]).start()

    def send_share(h):
        def one(step, carry):
            to = peer(step)
            cols = columns(to, h)
            for a, src in enumerate((q_hbm, k_hbm, v_hbm)):
                pltpu.make_async_remote_copy(
                    src_ref=src.at[own_rows, cols],
                    dst_ref=recv.at[h, me, a, own_rows],
                    send_sem=share_send.at[h],
                    recv_sem=share_recv.at[h],
                    device_id={"seq": to},
                    device_id_type=MESH,
                ).start()
            return carry

        lax.fori_loop(1, n, one, 0)

    def share_bytes(h):
        return recv.at[h, pl.ds(0, n - 1), pl.ds(0, 3), pl.ds(0, share)]

    def plane_bytes(h):
        return recv.at[h, pl.ds(0, n - 1), pl.ds(0, 3), pl.ds(0, (planes - 1) * share)]

    def forward(h):
        wait_bytes(share_bytes(h), share_recv.at[h])

        def one(step, carry):
            block = recv.at[h, peer(step), pl.ds(0, 3), own_rows]

            def over(hop, inner):
                pltpu.make_async_remote_copy(
                    src_ref=block,
                    dst_ref=block,
                    send_sem=plane_send.at[h],
                    recv_sem=plane_recv.at[h],
                    device_id={"rows": other_plane(hop)},
                    device_id_type=MESH,
                ).start()
                return inner

            return lax.fori_loop(1, planes, over, carry)

        lax.fori_loop(1, n, one, 0)

    def wait_bytes(ref, sem):
        pltpu.make_async_copy(ref, ref, sem).wait()

    def wait_sent(h):
        first = 0 if h == 0 else 3
        wait_bytes(recv.at[h, pl.ds(0, n - 1), pl.ds(first, 4 - first)], in_send.at[h])

    def wait_in(h, first):
        wait_bytes(recv.at[h, 0], in_local.at[h])
        wait_bytes(recv.at[h, pl.ds(0, n - 1), pl.ds(first, 4 - first)], in_recv.at[h])

    def send_query(h, to):
        cols = columns(me, h)

        @pl.when(to != me)
        def away():
            pltpu.make_async_remote_copy(
                src_ref=outs.at[h, to, 0],
                dst_ref=gq_hbm.at[0, :, cols],
                send_sem=out_send,
                recv_sem=out_recv,
                device_id={"seq": to},
                device_id_type=MESH,
            ).start()

        @pl.when(to == me)
        def here():
            pltpu.make_async_copy(outs.at[h, to, 0], gq_hbm.at[0, :, cols], out_local).start()

    def send_out(h):
        cols = columns(me, h)

        def one(step, carry):
            to = peer(step)
            for a, dst in ((1, gk_hbm), (2, gv_hbm)):
                pltpu.make_async_remote_copy(
                    src_ref=outs.at[h, to, a],
                    dst_ref=dst.at[0, :, cols],
                    send_sem=out_send,
                    recv_sem=out_recv,
                    device_id={"seq": to},
                    device_id_type=MESH,
                ).start()
            return carry

        lax.fori_loop(1, n, one, 0)
        for a, dst in ((1, gk_hbm), (2, gv_hbm)):
            pltpu.make_async_copy(outs.at[h, me, a], dst.at[0, :, cols], out_local).start()

    def attend(h):
        def turn(src, carry):
            at = pl.ds(pl.multiple_of(src * tok, tok), tok)
            kt_ref[:, at] = recv[h, src, 1].T
            vt_ref[:, at] = recv[h, src, 2].T
            return carry

        lax.fori_loop(0, n, turn, 0)
        dk_ref[...] = jnp.zeros_like(dk_ref)
        dv_ref[...] = jnp.zeros_like(dv_ref)
        rows = table_ref[:, columns(me, h)].astype(jnp.float32)
        picked = lax.broadcasted_iota(jnp.int32, rows.shape, 0) == residue_ref[0]
        added = jnp.sum(jnp.where(picked, rows, 0.0), axis=0, keepdims=True)

        def queries_of(group, place):
            spot = group * batch + place
            src = lax.rem(me + spot, n)
            cols = pl.ds(pl.multiple_of(place * tok, tok), tok)
            if heads > 2:

                @pl.when((h == 0) & (spot == min(3, n - 1)))
                def onward():
                    for later in range(2, heads):
                        forward(later)

            q = recv[h, src, 0]
            q_ref[cols, :] = q
            at = lax.broadcasted_iota(jnp.int32, (tok, D_HEAD), 0) + src * tok
            term = jnp.where(at == pos_ref[0], added, 0.0)
            cot = (recv[h, src, 3].astype(jnp.float32) + term).astype(jnp.bfloat16)
            top = jnp.full((8, tok), NEG, jnp.float32)
            for c in range(n):
                scores = lax.dot_general(recv[h, c, 1], q, nt, preferred_element_type=jnp.float32)
                for b in range(per):
                    part = scores[b * BLOCK : (b + 1) * BLOCK] + bias_ref[src, pl.ds(c * per + b, 1), :]
                    s_ref[c, b * BLOCK : (b + 1) * BLOCK, :] = part
                    top = jnp.maximum(top, jnp.max(part.reshape(BLOCK // 8, 8, tok), axis=0))
            top = jnp.max(top, axis=0, keepdims=True)
            total = jnp.zeros((8, tok), jnp.float32)
            for c in range(n):
                weights = jnp.exp2((s_ref[c] - top) * (scale * LOG2E))
                total += jnp.sum(weights.reshape(tok // 8, 8, tok), axis=0)
                w_ref[c, :, cols] = weights.astype(jnp.bfloat16)
            attended = lax.dot_general(
                vt_ref[...],
                w_ref[:, :, cols].reshape(n * tok, tok),
                nn,
                preferred_element_type=jnp.float32,
            )
            inverse = 1.0 / jnp.sum(total, axis=0, keepdims=True)
            cot_t = (cot.astype(jnp.float32).T * inverse).astype(jnp.bfloat16)
            cot_wide = cot_t.astype(jnp.float32)
            scaled_ref[cols, :] = cot_wide.T.astype(jnp.bfloat16)
            delta = inverse * jnp.sum(cot_wide * attended, axis=0, keepdims=True)
            for c in range(n):
                grad_probs = lax.dot_general(
                    recv[h, c, 2], cot_t, nn, preferred_element_type=jnp.float32
                )
                ds_ref[c, :, cols] = w_ref[c, :, cols] * (grad_probs - delta).astype(jnp.bfloat16)
            query_t = lax.dot_general(
                kt_ref[...],
                ds_ref[:, :, cols].reshape(n * tok, tok),
                nn,
                preferred_element_type=jnp.float32,
            )
            outs[h, src, 0] = (scale * query_t.T).astype(jnp.bfloat16)
            send_query(h, src)

        def batch_of(group, carry):
            def inner(place, unused):
                queries_of(group, place)
                return unused

            lax.fori_loop(0, batch, inner, 0)
            q_all = q_ref[...]
            cot_all = scaled_ref[...]

            def keys_of(c, unused):
                dv_ref[c] += lax.dot_general(
                    w_ref[c], cot_all, nn, preferred_element_type=jnp.float32
                )
                dk_ref[c] += lax.dot_general(ds_ref[c], q_all, nn, preferred_element_type=jnp.float32)
                return unused

            lax.fori_loop(0, n, keys_of, 0)
            return carry

        lax.fori_loop(0, n // batch, batch_of, 0)

        def close(src, carry):
            outs[h, src, 1] = (scale * dk_ref[src]).astype(jnp.bfloat16)
            outs[h, src, 2] = dv_ref[src].astype(jnp.bfloat16)
            return carry

        lax.fori_loop(0, n, close, 0)

    def mask_of(src, carry):
        for p in range(per):
            block = src * per + p
            ids = lax.broadcasted_iota(jnp.int32, (bias_ref.shape[1], BLOCK), 0)
            hit = ids == tiles_ref[block, 0]
            for j in range(1, tiles_ref.shape[1]):
                hit |= ids == jnp.where(j < counts_ref[block], tiles_ref[block, j], -1)
            bias_ref[src, :, p * BLOCK : (p + 1) * BLOCK] = jnp.where(hit, 0.0, NEG)
        return carry

    if heads > 1:
        send_share(1)
    send_in(0, 0)
    lax.fori_loop(0, n, mask_of, 0)
    if heads > 1:
        forward(1)
    wait_sent(0)
    for h in range(2, heads):
        send_share(h)
    for h in range(1, heads):
        send_in(h, 3)
    wait_in(0, 0)

    def turn_of(h, carry):
        @pl.when(h > 0)
        def arrived():
            wait_in(h, 3)
            wait_bytes(plane_bytes(h), plane_recv.at[h])

        attend(h)
        send_out(h)
        return carry

    lax.fori_loop(0, heads, turn_of, 0)
    for h in range(1, heads):
        wait_sent(h)
        wait_bytes(share_bytes(h), share_send.at[h])
        wait_bytes(plane_bytes(h), plane_send.at[h])
    wait_bytes(outs.at[:, pl.ds(0, n - 1)], out_send)
    wait_bytes(outs.at[:, pl.ds(0, n - 1)], out_recv)
    wait_bytes(outs.at[:, 0], out_local)


def hand_on(a_ref, b_ref, c_ref, a_out, b_out, c_out, sems):
    pairs = ((a_ref, a_out), (b_ref, b_out), (c_ref, c_out))
    copies = [pltpu.make_async_copy(src, dst, sems.at[i]) for i, (src, dst) in enumerate(pairs)]
    for copy in copies:
        copy.start()
    for copy in copies:
        copy.wait()


def per_device(queries, keys, values, grad_out, table, positions, residues, tiles, counts):
    n, planes = lax.axis_size("seq"), lax.axis_size("rows")
    tok, width = queries.shape
    heads = width // D_HEAD // n
    block_total = tiles.shape[0]
    batch = math.gcd(4, n)
    hbm = pl.BlockSpec(memory_space=pl.ANY)
    smem = pl.BlockSpec(memory_space=pltpu.SMEM)
    vmem = pl.BlockSpec(memory_space=pltpu.VMEM)
    shape = jax.ShapeDtypeStruct((1, tok, width), jnp.bfloat16)
    results = pl.pallas_call(
        functools.partial(fused_kernel, n, planes, heads),
        in_specs=[smem, smem, smem, smem, vmem, hbm, hbm, hbm, hbm],
        out_specs=[hbm] * 3,
        out_shape=[shape] * 3,
        scratch_shapes=[
            pltpu.VMEM((heads, n, 4, tok, D_HEAD), jnp.bfloat16),
            pltpu.VMEM((heads, n, 3, tok, D_HEAD), jnp.bfloat16),
            pltpu.VMEM((n, block_total, tok), jnp.float32),
            pltpu.VMEM((D_HEAD, n * tok), jnp.bfloat16),
            pltpu.VMEM((D_HEAD, n * tok), jnp.bfloat16),
            pltpu.VMEM((n, tok, tok), jnp.float32),
            pltpu.VMEM((n, tok, batch * tok), jnp.bfloat16),
            pltpu.VMEM((n, tok, batch * tok), jnp.bfloat16),
            pltpu.VMEM((batch * tok, D_HEAD), jnp.bfloat16),
            pltpu.VMEM((batch * tok, D_HEAD), jnp.bfloat16),
            pltpu.VMEM((n, tok, D_HEAD), jnp.float32),
            pltpu.VMEM((n, tok, D_HEAD), jnp.float32),
            pltpu.SemaphoreType.DMA((heads,)),
            pltpu.SemaphoreType.DMA((heads,)),
            pltpu.SemaphoreType.DMA((heads,)),
            pltpu.SemaphoreType.DMA((heads,)),
            pltpu.SemaphoreType.DMA((heads,)),
            pltpu.SemaphoreType.DMA((heads,)),
            pltpu.SemaphoreType.DMA((heads,)),
            pltpu.SemaphoreType.DMA,
            pltpu.SemaphoreType.DMA,
            pltpu.SemaphoreType.DMA,
        ],
        compiler_params=pltpu.CompilerParams(
            vmem_limit_bytes=VMEM_LIMIT, collective_id=0, has_side_effects=True
        ),
        name="fused",
    )(positions, residues, tiles, counts, table, queries, keys, values, grad_out)
    return pl.pallas_call(
        hand_on,
        in_specs=[hbm] * 3,
        out_specs=[hbm] * 3,
        out_shape=[shape] * 3,
        scratch_shapes=[pltpu.SemaphoreType.DMA((3,))],
        name="hand_on",
    )(*results)


def solution(mesh):
    placed = (
        P("seq", None),
        P("seq", None),
        P("seq", None),
        P("rows", "seq", None),
        P(),
        P("rows"),
        P("rows"),
        P(),
        P(),
    )
    return jax.shard_map(
        per_device,
        mesh=mesh,
        in_specs=placed,
        out_specs=(P("rows", "seq", None), P("rows", "seq", None), P("rows", "seq", None)),
        check_vma=False,
    )
```

```python
import functools

import jax
import jax.numpy as jnp
from jax import lax
from jax.experimental import pallas as pl
from jax.experimental.pallas import tpu as pltpu
from jax.sharding import PartitionSpec as P

D_HEAD = 128
BLOCK = 128
NEG = -1e30
LOG2E = 1.4426950408889634
VMEM_LIMIT = 60 * 1024 * 1024
MESH = pl.DeviceIdType.MESH


def fused_kernel(
    n,
    planes,
    heads,
    pos_ref,
    residue_ref,
    tiles_ref,
    counts_ref,
    table_ref,
    q_hbm,
    k_hbm,
    v_hbm,
    g_hbm,
    gq_hbm,
    gk_hbm,
    gv_hbm,
    recv,
    outs,
    bias_ref,
    kt_ref,
    vt_ref,
    s_ref,
    w_ref,
    dk_ref,
    dv_ref,
    in_send,
    in_recv,
    in_local,
    share_send,
    share_recv,
    plane_send,
    plane_recv,
    out_send,
    out_recv,
    out_local,
):
    me = lax.axis_index("seq")
    tok = q_hbm.shape[0]
    per = tok // BLOCK
    scale = D_HEAD ** (-0.5)
    nt = (((1,), (1,)), ((), ()))
    nn = (((1,), (0,)), ((), ()))

    plane = lax.axis_index("rows")
    share = tok // planes
    own_rows = pl.ds(pl.multiple_of(plane * share, share), share)
    core = lax.rem(me, 2)

    def peer(step):
        high, mid, low = step // 4, (step // 2) % 2, step % 2
        swapped = (high // 2) * 8 + mid * 4 + (high % 2) * 2 + low
        off = step + core * (swapped - step)
        return (
            ((me // 4 + off // 4) % (n // 4)) * 4
            + ((me // 2 + off // 2) % 2) * 2
            + (me + off) % 2
        )

    def other_plane(step):
        return lax.rem(plane + step, planes)

    barrier = pltpu.get_barrier_semaphore()

    def greet(step, carry):
        pl.semaphore_signal(barrier, inc=1, device_id={"seq": peer(step)}, device_id_type=MESH)
        return carry

    def greet_plane(step, carry):
        to = other_plane(step)
        pl.semaphore_signal(barrier, inc=1, device_id={"rows": to}, device_id_type=MESH)
        return carry

    lax.fori_loop(1, n, greet, 0)
    lax.fori_loop(1, planes, greet_plane, 0)
    pl.semaphore_wait(barrier, n - 1 + planes - 1)

    def columns(owner, h):
        return pl.ds(pl.multiple_of((owner * heads + h) * D_HEAD, D_HEAD), D_HEAD)

    def sources(cols):
        return (q_hbm.at[:, cols], k_hbm.at[:, cols], v_hbm.at[:, cols], g_hbm.at[0, :, cols])

    def send_in(h, first):
        def one(step, carry):
            to = peer(step)
            for a, src in enumerate(sources(columns(to, h))):
                if a >= first:
                    pltpu.make_async_remote_copy(
                        src_ref=src,
                        dst_ref=recv.at[h, me, a],
                        send_sem=in_send.at[h],
                        recv_sem=in_recv.at[h],
                        device_id={"seq": to},
                        device_id_type=MESH,
                    ).start()
            return carry

        lax.fori_loop(1, n, one, 0)
        for a, src in enumerate(sources(columns(me, h))):
            pltpu.make_async_copy(src, recv.at[h, me, a], in_local.at[h]).start()

    def send_share(h):
        def one(step, carry):
            to = peer(step)
            cols = columns(to, h)
            for a, src in enumerate((q_hbm, k_hbm, v_hbm)):
                pltpu.make_async_remote_copy(
                    src_ref=src.at[own_rows, cols],
                    dst_ref=recv.at[h, me, a, own_rows],
                    send_sem=share_send.at[h],
                    recv_sem=share_recv.at[h],
                    device_id={"seq": to},
                    device_id_type=MESH,
                ).start()
            return carry

        lax.fori_loop(1, n, one, 0)

    def share_bytes(h):
        return recv.at[h, pl.ds(0, n - 1), pl.ds(0, 3), pl.ds(0, share)]

    def plane_bytes(h):
        return recv.at[h, pl.ds(0, n - 1), pl.ds(0, 3), pl.ds(0, (planes - 1) * share)]

    def forward(h):
        wait_bytes(share_bytes(h), share_recv.at[h])

        def one(step, carry):
            block = recv.at[h, peer(step), pl.ds(0, 3), own_rows]

            def over(hop, inner):
                pltpu.make_async_remote_copy(
                    src_ref=block,
                    dst_ref=block,
                    send_sem=plane_send.at[h],
                    recv_sem=plane_recv.at[h],
                    device_id={"rows": other_plane(hop)},
                    device_id_type=MESH,
                ).start()
                return inner

            return lax.fori_loop(1, planes, over, carry)

        lax.fori_loop(1, n, one, 0)

    def wait_bytes(ref, sem):
        pltpu.make_async_copy(ref, ref, sem).wait()

    def wait_sent(h):
        first = 0 if h == 0 else 3
        wait_bytes(recv.at[h, pl.ds(0, n - 1), pl.ds(first, 4 - first)], in_send.at[h])

    def wait_in(h, first):
        wait_bytes(recv.at[h, 0], in_local.at[h])
        wait_bytes(recv.at[h, pl.ds(0, n - 1), pl.ds(first, 4 - first)], in_recv.at[h])

    def send_query(h, to):
        cols = columns(me, h)

        @pl.when(to != me)
        def away():
            pltpu.make_async_remote_copy(
                src_ref=outs.at[h, to, 0],
                dst_ref=gq_hbm.at[0, :, cols],
                send_sem=out_send,
                recv_sem=out_recv,
                device_id={"seq": to},
                device_id_type=MESH,
            ).start()

        @pl.when(to == me)
        def here():
            pltpu.make_async_copy(outs.at[h, to, 0], gq_hbm.at[0, :, cols], out_local).start()

    def send_out(h):
        cols = columns(me, h)

        def one(step, carry):
            to = peer(step)
            for a, dst in ((1, gk_hbm), (2, gv_hbm)):
                pltpu.make_async_remote_copy(
                    src_ref=outs.at[h, to, a],
                    dst_ref=dst.at[0, :, cols],
                    send_sem=out_send,
                    recv_sem=out_recv,
                    device_id={"seq": to},
                    device_id_type=MESH,
                ).start()
            return carry

        lax.fori_loop(1, n, one, 0)
        for a, dst in ((1, gk_hbm), (2, gv_hbm)):
            pltpu.make_async_copy(outs.at[h, me, a], dst.at[0, :, cols], out_local).start()

    def attend(h):
        def turn(src, carry):
            kt_ref[src] = recv[h, src, 1].T
            vt_ref[src] = recv[h, src, 2].T
            return carry

        lax.fori_loop(0, n, turn, 0)
        dk_ref[...] = jnp.zeros_like(dk_ref)
        dv_ref[...] = jnp.zeros_like(dv_ref)
        rows = table_ref[:, columns(me, h)].astype(jnp.float32)
        picked = lax.broadcasted_iota(jnp.int32, rows.shape, 0) == residue_ref[0]
        added = jnp.sum(jnp.where(picked, rows, 0.0), axis=0, keepdims=True)

        def queries_of(spot, carry):
            src = lax.rem(me + spot, n)
            if heads > 2:

                @pl.when((h == 0) & (spot == min(3, n - 1)))
                def onward():
                    for later in range(2, heads):
                        forward(later)

            q = recv[h, src, 0]
            at = lax.broadcasted_iota(jnp.int32, (tok, D_HEAD), 0) + src * tok
            term = jnp.where(at == pos_ref[0], added, 0.0)
            cot = (recv[h, src, 3].astype(jnp.float32) + term).astype(jnp.bfloat16)
            top = jnp.full((1, tok), NEG, jnp.float32)
            for c in range(n):
                scores = lax.dot_general(recv[h, c, 1], q, nt, preferred_element_type=jnp.float32)
                for b in range(per):
                    part = scores[b * BLOCK : (b + 1) * BLOCK] + bias_ref[src, pl.ds(c * per + b, 1), :]
                    s_ref[c, b * BLOCK : (b + 1) * BLOCK, :] = part
                    top = jnp.maximum(top, jnp.max(part, axis=0, keepdims=True))
            total = jnp.zeros((1, tok), jnp.float32)
            attended = jnp.zeros((D_HEAD, tok), jnp.float32)
            for c in range(n):
                weights = jnp.exp2((s_ref[c] - top) * (scale * LOG2E))
                total += jnp.sum(weights, axis=0, keepdims=True)
                weights_bf = weights.astype(jnp.bfloat16)
                w_ref[c] = weights_bf
                attended += lax.dot_general(
                    vt_ref[c], weights_bf, nn, preferred_element_type=jnp.float32
                )
            inverse = 1.0 / total
            cot_t = (cot.astype(jnp.float32).T * inverse).astype(jnp.bfloat16)
            cot_wide = cot_t.astype(jnp.float32)
            scaled = cot_wide.T.astype(jnp.bfloat16)
            delta = inverse * jnp.sum(cot_wide * attended, axis=0, keepdims=True)
            query_t = jnp.zeros((D_HEAD, tok), jnp.float32)
            for c in range(n):
                grad_probs = lax.dot_general(
                    recv[h, c, 2], cot_t, nn, preferred_element_type=jnp.float32
                )
                weights_bf = w_ref[c]
                grad_scores = weights_bf * (grad_probs - delta).astype(jnp.bfloat16)
                dv_ref[c] += lax.dot_general(
                    weights_bf, scaled, nn, preferred_element_type=jnp.float32
                )
                dk_ref[c] += lax.dot_general(grad_scores, q, nn, preferred_element_type=jnp.float32)
                query_t += lax.dot_general(
                    kt_ref[c], grad_scores, nn, preferred_element_type=jnp.float32
                )
            outs[h, src, 0] = (scale * query_t.T).astype(jnp.bfloat16)
            send_query(h, src)
            return carry

        lax.fori_loop(0, n, queries_of, 0)

        def close(src, carry):
            outs[h, src, 1] = (scale * dk_ref[src]).astype(jnp.bfloat16)
            outs[h, src, 2] = dv_ref[src].astype(jnp.bfloat16)
            return carry

        lax.fori_loop(0, n, close, 0)

    def mask_of(src, carry):
        for p in range(per):
            block = src * per + p
            ids = lax.broadcasted_iota(jnp.int32, (bias_ref.shape[1], BLOCK), 0)
            hit = ids == tiles_ref[block, 0]
            for j in range(1, tiles_ref.shape[1]):
                hit |= ids == jnp.where(j < counts_ref[block], tiles_ref[block, j], -1)
            bias_ref[src, :, p * BLOCK : (p + 1) * BLOCK] = jnp.where(hit, 0.0, NEG)
        return carry

    if heads > 1:
        send_share(1)
    send_in(0, 0)
    lax.fori_loop(0, n, mask_of, 0)
    if heads > 1:
        forward(1)
    wait_sent(0)
    for h in range(2, heads):
        send_share(h)
    for h in range(1, heads):
        send_in(h, 3)
    wait_in(0, 0)

    def turn_of(h, carry):
        @pl.when(h > 0)
        def arrived():
            wait_in(h, 3)
            wait_bytes(plane_bytes(h), plane_recv.at[h])

        attend(h)
        send_out(h)
        return carry

    lax.fori_loop(0, heads, turn_of, 0)
    for h in range(1, heads):
        wait_sent(h)
        wait_bytes(share_bytes(h), share_send.at[h])
        wait_bytes(plane_bytes(h), plane_send.at[h])
    wait_bytes(outs.at[:, pl.ds(0, n - 1)], out_send)
    wait_bytes(outs.at[:, pl.ds(0, n - 1)], out_recv)
    wait_bytes(outs.at[:, 0], out_local)


def per_device(queries, keys, values, grad_out, table, positions, residues, tiles, counts):
    n, planes = lax.axis_size("seq"), lax.axis_size("rows")
    tok, width = queries.shape
    heads = width // D_HEAD // n
    block_total = tiles.shape[0]
    hbm = pl.BlockSpec(memory_space=pl.ANY)
    smem = pl.BlockSpec(memory_space=pltpu.SMEM)
    vmem = pl.BlockSpec(memory_space=pltpu.VMEM)
    shape = jax.ShapeDtypeStruct((1, tok, width), jnp.bfloat16)
    return pl.pallas_call(
        functools.partial(fused_kernel, n, planes, heads),
        in_specs=[smem, smem, smem, smem, vmem, hbm, hbm, hbm, hbm],
        out_specs=[hbm] * 3,
        out_shape=[shape] * 3,
        scratch_shapes=[
            pltpu.VMEM((heads, n, 4, tok, D_HEAD), jnp.bfloat16),
            pltpu.VMEM((heads, n, 3, tok, D_HEAD), jnp.bfloat16),
            pltpu.VMEM((n, block_total, tok), jnp.float32),
            pltpu.VMEM((n, D_HEAD, tok), jnp.bfloat16),
            pltpu.VMEM((n, D_HEAD, tok), jnp.bfloat16),
            pltpu.VMEM((n, tok, tok), jnp.float32),
            pltpu.VMEM((n, tok, tok), jnp.bfloat16),
            pltpu.VMEM((n, tok, D_HEAD), jnp.float32),
            pltpu.VMEM((n, tok, D_HEAD), jnp.float32),
            pltpu.SemaphoreType.DMA((heads,)),
            pltpu.SemaphoreType.DMA((heads,)),
            pltpu.SemaphoreType.DMA((heads,)),
            pltpu.SemaphoreType.DMA((heads,)),
            pltpu.SemaphoreType.DMA((heads,)),
            pltpu.SemaphoreType.DMA((heads,)),
            pltpu.SemaphoreType.DMA((heads,)),
            pltpu.SemaphoreType.DMA,
            pltpu.SemaphoreType.DMA,
            pltpu.SemaphoreType.DMA,
        ],
        compiler_params=pltpu.CompilerParams(
            vmem_limit_bytes=VMEM_LIMIT, collective_id=0, has_side_effects=True
        ),
        name="fused",
    )(positions, residues, tiles, counts, table, queries, keys, values, grad_out)


def solution(mesh):
    placed = (
        P("seq", None),
        P("seq", None),
        P("seq", None),
        P("rows", "seq", None),
        P(),
        P("rows"),
        P("rows"),
        P(),
        P(),
    )
    return jax.shard_map(
        per_device,
        mesh=mesh,
        in_specs=placed,
        out_specs=(P("rows", "seq", None), P("rows", "seq", None), P("rows", "seq", None)),
        check_vma=False,
    )
```
